128 devices in a mesh: group: 2 (over z_hi), dev: 64 (over x, z_lo, y, core).
Axes of the slice: x: 4, y: 4, z: 4 (z_hi: 2, z_lo: 2; z = z_hi * 2 + z_lo), core: 2. Of those that a mesh axis runs over, the one named last changes fastest.
Arguments:
- new_weights: bfloat16 [64, 3584, 1024], P(None, ('group', 'dev')), may hold values from -80 to 80
- owner_map: int32 [64], replicated, may hold values from 0 to 63, each once
- block_mask: int32 [64, 28, 8], replicated, may hold values from 0 to 1, as said below
- base_codes: bfloat16 [64, 3584, 1024], P('dev'), may hold values from -8 to 7, as said below
- base_scale: float32 [64, 28, 8], P('dev'), may hold values from 0.05 to 0.4
Outputs:
- delta_blocks: bfloat16 [2, 64, 3584, 1024], P('group', 'dev')
- delta_scales: bfloat16 [2, 64, 28, 8], P('group', 'dev')
The draws below stay inside these ranges and needn't reach their ends.
Inputs may be any that keep to these rules, and one draw needn't show every extreme that they name: `base_codes`: whole numbers. `block_mask`: of each expert, every block row (a fixed a) holds exactly 4 ones.
All inputs are finite; a program needn't handle non-finite values.
Results may differ from the reference program's by a relative error of at most 0.001.
Values may be sent and summed in bfloat16 or wider, within the bound.
A program may use at most 128 MiB of HBM per device.

```python
import math
import jax
import jax.numpy as jnp
from jax import lax

D = 3584
FF = 1024
BLOCK = 128
PER_ROW = 4
EXPERTS = 64
N_GROUP = 2


def draw_new_weights(key, part):
    key = jax.random.fold_in(key, 11)
    keys = jax.random.split(key, 3)
    row_scale = jnp.exp(jax.random.uniform(keys[0], (EXPERTS, D, 1), jnp.float32, math.log(0.3), math.log(3.0)))
    col_scale = jnp.exp(jax.random.uniform(keys[1], (EXPERTS, 1, FF), jnp.float32, math.log(0.3), math.log(3.0)))
    values = jax.random.normal(keys[2], (EXPERTS, D, FF), jnp.float32) * row_scale * col_scale
    values = jnp.clip(values, -80.0, 80.0)
    return values.astype(jnp.bfloat16)


def draw_base_codes(key, part):
    key = jax.random.fold_in(key, 23)
    codes = jax.random.randint(key, (EXPERTS, D, FF), -8, 8, jnp.int32)
    return codes.astype(jnp.float32).astype(jnp.bfloat16)


def draw_block_mask(key, part):
    key = jax.random.fold_in(key, 37)
    col_blocks = FF // BLOCK
    keys = jax.random.split(key, EXPERTS * (D // BLOCK))
    ranks = jax.vmap(lambda single: jax.random.permutation(single, col_blocks))(keys)
    chosen = (ranks < PER_ROW).astype(jnp.int32)
    return chosen.reshape(EXPERTS, D // BLOCK, col_blocks)


def shard_levels(rng, extent, shards, smallest, high):
    gain = 1.0
    for dim, parts in shards:
        draws = jax.random.uniform(jax.random.fold_in(jax.random.fold_in(rng, 6), dim), (parts,), jnp.float32, smallest / len(shards), high / len(shards))
        gain = gain * jnp.repeat(jnp.exp(draws), extent[dim] // parts).reshape((-1,) + (1,) * (len(extent) - 1 - dim))
    return gain


def setup_inputs(seed: int = 0) -> dict:
    seeds = jax.random.split(jax.random.key(seed), 6)
    new_weights = draw_new_weights(jax.random.fold_in(seeds[5], 71), 0)
    owner_map = jax.random.permutation(seeds[1], EXPERTS).astype(jnp.int32)
    block_mask = draw_block_mask(jax.random.fold_in(seeds[5], 71), 0)
    base_codes = draw_base_codes(jax.random.fold_in(seeds[5], 71), 0)
    base_scale = jnp.clip(jnp.exp(math.log(0.4) - 2.0794415 * jax.random.uniform(seeds[4], (EXPERTS, D // BLOCK, FF // BLOCK), jnp.float32) ** shard_levels(seeds[4], (EXPERTS, D // BLOCK, FF // BLOCK), ((0, 64),), -0.2, 0.2)), 0.05, 0.4)
    return {"new_weights": new_weights, "owner_map": owner_map, "block_mask": block_mask, "base_codes": base_codes, "base_scale": base_scale}


def encode(updated, codes, scale, mask):
    row_blocks, col_blocks = scale.shape
    base_vals = codes.astype(jnp.float32).reshape(row_blocks, BLOCK, col_blocks, BLOCK) * scale[:, None, :, None]
    change = updated.astype(jnp.float32).reshape(row_blocks, BLOCK, col_blocks, BLOCK) - base_vals
    peak_abs = jnp.max(jnp.abs(change), axis=(1, 3)) + 1e-6
    carries = mask[:, None, :, None] > 0
    scaled = jnp.where(carries, change / peak_abs[:, None, :, None], 0.0).astype(jnp.bfloat16)
    scaled = scaled.reshape(row_blocks * BLOCK, col_blocks * BLOCK)
    block_scales = jnp.where(mask > 0, peak_abs, 0.0).astype(jnp.bfloat16)
    return scaled, block_scales


def reference(new_weights, owner_map, block_mask, base_codes, base_scale):
    owners = jnp.arange(EXPERTS, dtype=jnp.int32)
    holder = jnp.sum(jnp.where(owner_map[:, None] == owners[None, :], owners[:, None], 0), axis=0).astype(jnp.int32)

    def encode_owner(slot_index):
        expert = holder[slot_index]
        updated = lax.dynamic_index_in_dim(new_weights, expert, 0, keepdims=False)
        mask_rows = lax.dynamic_index_in_dim(block_mask, expert, 0, keepdims=False)
        codes = lax.dynamic_index_in_dim(base_codes, slot_index, 0, keepdims=False)
        scale = lax.dynamic_index_in_dim(base_scale, slot_index, 0, keepdims=False)
        return encode(updated, codes, scale, mask_rows)

    delta_blocks, delta_scales = lax.map(encode_owner, owners)
    delta_blocks = jnp.broadcast_to(delta_blocks[None], (N_GROUP,) + delta_blocks.shape)
    delta_scales = jnp.broadcast_to(delta_scales[None], (N_GROUP,) + delta_scales.shape)
    return delta_blocks, delta_scales
```

```python
import jax
import jax.numpy as jnp
from jax import lax
from jax.experimental import pallas as pl
from jax.experimental.pallas import tpu as pltpu
from jax.sharding import PartitionSpec as P

BLOCK = 128
MESH = pl.DeviceIdType.MESH
OWNERS = 64
GROUPS = 2
SHARD = 28
ROW_BLOCKS = 28
COL_BLOCKS = 8
CARRIED = 4
MAIN = 24
PIECE = SHARD * CARRIED


def owner_at(me, t):
    core, y, zl, x = me % 2, (me // 2) % 4, (me // 8) % 2, me // 16
    a, b, e = t % 4, (t // 4) % 4, t // 16
    v = (a + b + e) % 4
    x = (x + a) % 4
    y = (y + a + b) % 4
    zl = (zl + v) % 2
    core = (core + v // 2) % 2
    return ((x * 2 + zl) * 4 + y) * 2 + core


def exchange(holder, places, weights, recv, mine, send, load_sem, own_sem, send_sem, recv_sem):
    g = lax.axis_index("group")
    me = lax.axis_index("dev")
    my_id = g * OWNERS + me

    barrier = pltpu.get_barrier_semaphore()

    def greet(i, carry):
        other = (my_id + i) % (GROUPS * OWNERS)
        pl.semaphore_signal(
            barrier, inc=1, device_id=(other // OWNERS, other % OWNERS), device_id_type=MESH
        )
        return carry

    loads = [
        pltpu.make_async_copy(
            weights.at[:, :, pl.ds(BLOCK * c, BLOCK)], mine.at[c], load_sem.at[c]
        )
        for c in range(COL_BLOCKS)
    ]
    for load in loads:
        load.start()
    lax.fori_loop(1, GROUPS * OWNERS, greet, 0)
    for load in loads:
        load.wait()

    first_row = my_id * SHARD
    block_a = first_row // BLOCK
    block_b = jnp.minimum(block_a + 1, ROW_BLOCKS - 1)
    split = (block_a + 1) * BLOCK - first_row
    phase = me % 2
    row = lax.broadcasted_iota(jnp.int32, (SHARD, BLOCK), 0)
    in_a = row < split
    sub = lax.broadcasted_iota(jnp.int32, (8, BLOCK), 0)
    straight = (sub // 4) == phase

    def pack(t):
        e = holder[owner_at(me, t)]
        code_a = places[e, block_a]
        code_b = places[e, block_b]
        mains, rests = [], []
        for k in range(CARRIED):
            rows_a = mine[(code_a >> (3 * k)) & 7, e].astype(jnp.float32)
            rows_b = mine[(code_b >> (3 * k)) & 7, e].astype(jnp.float32)
            rows = jnp.where(in_a, rows_a, rows_b)
            rows = jnp.concatenate([rows, jnp.zeros((4, BLOCK), jnp.float32)], axis=0)
            rows = jnp.where(phase == 1, jnp.roll(rows, -4, axis=0), rows)
            mains.append(rows[:MAIN])
            rests.append(rows[MAIN:])
        left_a = jnp.where(straight, rests[0], jnp.roll(rests[1], 4, axis=0))
        left_b = jnp.where(straight, rests[2], jnp.roll(rests[3], 4, axis=0))
        send[t] = jnp.concatenate(mains + [left_a, left_b], axis=0).astype(jnp.bfloat16)

    def to(t, gt):
        return pltpu.make_async_remote_copy(
            src_ref=send.at[t],
            dst_ref=recv.at[my_id],
            send_sem=send_sem,
            recv_sem=recv_sem,
            device_id=(gt, owner_at(me, t)),
            device_id_type=MESH,
        )

    pack(0)
    keep = pltpu.make_async_copy(send.at[0], recv.at[my_id], own_sem)
    keep.start()
    pl.semaphore_wait(barrier, GROUPS * OWNERS - 1)
    to(0, 1 - g).start()

    def step(t, carry):
        pack(t)
        to(t, g).start()
        to(t, 1 - g).start()
        return carry

    lax.fori_loop(1, OWNERS, step, 0)

    keep.wait()
    sent = recv.at[pl.ds(0, GROUPS * OWNERS - 1)]
    pltpu.make_async_copy(sent, sent, send_sem).wait()
    pltpu.make_async_copy(sent, sent, recv_sem).wait()


def decode(places, scales, recv, codes, out, out_scales):
    group = pl.program_id(0)
    sub = lax.broadcasted_iota(jnp.int32, (8, BLOCK), 0)
    low = sub < 4
    lane = lax.broadcasted_iota(jnp.int32, (1, BLOCK), 1)
    per = ROW_BLOCKS // 4
    out[...] = jnp.zeros_like(out)

    def pair_rows(m, k):
        even = recv[2 * m].astype(jnp.float32)
        odd = recv[2 * m + 1].astype(jnp.float32)
        at = CARRIED * MAIN + 8 * (k // 2)
        rest_even, rest_odd = even[at : at + 8], odd[at : at + 8]
        if k % 2 == 0:
            middle = jnp.where(low, rest_even, rest_odd)
        else:
            middle = jnp.roll(jnp.where(low, rest_odd, rest_even), 4, axis=0)
        return [even[MAIN * k : MAIN * (k + 1)], middle, odd[MAIN * k : MAIN * (k + 1)]]

    for r in range(per):
        a = group * per + r
        code = places[a]
        scale_row = jnp.zeros((1, BLOCK), jnp.float32)
        for k in range(CARRIED):
            rows = []
            first, last = BLOCK * r, BLOCK * (r + 1)
            for m in range(first // 56, (last + 55) // 56):
                whole = jnp.concatenate(pair_rows(m, k), axis=0)
                rows.append(whole[max(first - 56 * m, 0) : min(last - 56 * m, 56)])
            updated = jnp.concatenate(rows, axis=0)
            col = (code >> (3 * k)) & 7
            at = pl.ds(pl.multiple_of(col * BLOCK, BLOCK), BLOCK)
            here = pl.ds(BLOCK * r, BLOCK)
            change = updated - codes[here, at].astype(jnp.float32) * scales[a, col]
            peak = jnp.max(jnp.max(jnp.abs(change), axis=0, keepdims=True), axis=1, keepdims=True) + 1e-06
            out[here, at] = (change * (1.0 / peak)).astype(jnp.bfloat16)
            scale_row = jnp.where(lane == col, peak, scale_row)
        out_scales[pl.ds(a, 1), :] = scale_row[:, :COL_BLOCKS]


def body(new_weights, owner_map, block_mask, base_codes, base_scale):
    owners = jnp.arange(OWNERS, dtype=jnp.int32)
    holder = jnp.sum(jnp.where(owner_map[:, None] == owners[None, :], owners[:, None], 0), axis=0)
    carried = block_mask > 0
    upto = jnp.zeros(carried.shape[:2], jnp.int32)
    places = jnp.zeros(carried.shape[:2], jnp.int32)
    for c in range(COL_BLOCKS):
        here = carried[:, :, c]
        places = places + jnp.where(here, c << upto, 0)
        upto = upto + jnp.where(here, 3, 0)

    recv = pl.pallas_call(
        exchange,
        out_shape=jax.ShapeDtypeStruct((GROUPS * OWNERS, PIECE, BLOCK), jnp.bfloat16),
        in_specs=[
            pl.BlockSpec(memory_space=pltpu.SMEM),
            pl.BlockSpec(memory_space=pltpu.SMEM),
            pl.BlockSpec(memory_space=pl.ANY),
        ],
        out_specs=pl.BlockSpec(memory_space=pl.ANY),
        scratch_shapes=[
            pltpu.VMEM((COL_BLOCKS, OWNERS, SHARD, BLOCK), jnp.bfloat16),
            pltpu.VMEM((OWNERS, PIECE, BLOCK), jnp.bfloat16),
            pltpu.SemaphoreType.DMA((COL_BLOCKS,)),
            pltpu.SemaphoreType.DMA,
            pltpu.SemaphoreType.DMA,
            pltpu.SemaphoreType.DMA,
        ],
        compiler_params=pltpu.CompilerParams(
            collective_id=0, has_side_effects=True, vmem_limit_bytes=32 * 2**20
        ),
        name="exchange",
    )(holder, places, new_weights)

    own = places[holder[lax.axis_index("dev")]]
    per = ROW_BLOCKS // 4
    deltas, scales = pl.pallas_call(
        decode,
        grid=(4,),
        out_shape=(
            jax.ShapeDtypeStruct(base_codes.shape[1:], jnp.bfloat16),
            jax.ShapeDtypeStruct((ROW_BLOCKS, COL_BLOCKS), jnp.float32),
        ),
        in_specs=[
            pl.BlockSpec(memory_space=pltpu.SMEM),
            pl.BlockSpec(memory_space=pltpu.SMEM),
            pl.BlockSpec((32, PIECE, BLOCK), lambda i: (i, 0, 0)),
            pl.BlockSpec((per * BLOCK, COL_BLOCKS * BLOCK), lambda i: (i, 0)),
        ],
        out_specs=(
            pl.BlockSpec((per * BLOCK, COL_BLOCKS * BLOCK), lambda i: (i, 0)),
            pl.BlockSpec((ROW_BLOCKS, COL_BLOCKS), lambda i: (0, 0)),
        ),
        compiler_params=pltpu.CompilerParams(vmem_limit_bytes=48 * 2**20),
        name="decode",
    )(own, base_scale[0], recv, base_codes[0])
    return deltas[None, None], scales.astype(jnp.bfloat16)[None, None]


def solution(mesh):
    return jax.shard_map(
        body,
        mesh=mesh,
        in_specs=(
            P(None, ("group", "dev"), None),
            P(),
            P(),
            P("dev", None, None),
            P("dev", None, None),
        ),
        out_specs=(P("group", "dev", None, None), P("group", "dev", None, None)),
        check_vma=False,
    )
```

```python
import jax
import jax.numpy as jnp
from jax import lax
from jax.experimental import pallas as pl
from jax.experimental.pallas import tpu as pltpu
from jax.sharding import PartitionSpec as P

BLOCK = 128
MESH = pl.DeviceIdType.MESH
OWNERS = 64
GROUPS = 2
PEERS = GROUPS * OWNERS - 1
SHARD = 28
ROW_BLOCKS = 28
COL_BLOCKS = 8
CARRIED = 4
MAIN = 24
PIECE = SHARD * CARRIED
PAIR = 2 * SHARD
SETS = 4
PER_SET = ROW_BLOCKS // SETS
CHUNKS = 7
CHUNK = 4 * OWNERS
HALF = OWNERS // 2


def owner_at(me, t):
    core, y, zl, x = me % 2, (me // 2) % 4, (me // 8) % 2, me // 16
    a, b, e = t % 4, (t // 4) % 4, t // 16
    v = (a + b + e) % 4
    x = (x + a) % 4
    y = (y + a + b) % 4
    zl = (zl + v) % 2
    core = (core + v // 2) % 2
    return ((x * 2 + zl) * 4 + y) * 2 + core


def places_of(mask):
    axis = mask.ndim - 2
    column = lax.broadcasted_iota(jnp.int32, mask.shape, axis)
    upto = mask
    for step in (1, 2, 4):
        upto = upto + jnp.where(column >= step, pltpu.roll(upto, step, axis), 0)
    value = jnp.zeros_like(mask)
    for k in range(CARRIED):
        value = value + jnp.where(upto == k + 1, column << (3 * k), 0)
    return jnp.sum(jnp.where(mask > 0, value, 0), axis=axis, keepdims=True)


def column_of(code, k):
    return (code >> (3 * k)) & 7


def exchange(
    owner_map, mask, scales, codes, weights, recv, own, scales_out, codes_out,
    owners, masks, tile, table, raw, by_expert, turn, turn_rest, send,
    small_sems, load_sems, keep_sem, send_sem, recv_sem,
):
    g = lax.axis_index("group")
    me = lax.axis_index("dev")
    my_id = g * OWNERS + me
    first_row = my_id * SHARD
    block_a = first_row // BLOCK
    block_b = jnp.minimum(block_a + 1, ROW_BLOCKS - 1)
    split = (block_a + 1) * BLOCK - first_row
    phase = me % 2

    barrier = pltpu.get_barrier_semaphore()

    def greet(i, carry):
        other = (my_id + i) % (GROUPS * OWNERS)
        pl.semaphore_signal(
            barrier, inc=1, device_id=(other // OWNERS, other % OWNERS), device_id_type=MESH
        )
        return carry

    def load(i):
        rows = pl.ds(pl.multiple_of(i * CHUNK, CHUNK), CHUNK)
        return pltpu.make_async_copy(weights.at[rows], raw.at[rows], load_sems.at[i])

    load_owners = pltpu.make_async_copy(owner_map, owners, small_sems.at[0])
    load_masks = pltpu.make_async_copy(mask, masks, small_sems.at[1])
    load_scales = pltpu.make_async_copy(scales, scales_out, small_sems.at[2])
    load_codes = pltpu.make_async_copy(codes, codes_out, small_sems.at[4])
    load_owners.start()
    load_masks.start()
    for i in range(CHUNKS):
        load(i).start()
    lax.fori_loop(1, GROUPS * OWNERS, greet, 0)
    load_scales.start()
    load_codes.start()

    to_row = lax.broadcasted_iota(jnp.int32, (256, 256), 0)
    from_row = lax.broadcasted_iota(jnp.int32, (256, 256), 1)
    same = (to_row // 8 == from_row % HALF) & (to_row % 8 == from_row // HALF)
    turn[...] = jnp.where(same, 1.0, 0.0).astype(jnp.bfloat16)
    same = (to_row // 8 == from_row % HALF) & (to_row % 8 == from_row // HALF + 4 * phase)
    turn_rest[...] = jnp.where(same, 1.0, 0.0).astype(jnp.bfloat16)[:, :BLOCK]

    load_owners.wait()
    sub = lax.broadcasted_iota(jnp.int32, (OWNERS, OWNERS), 0)
    lane = lax.broadcasted_iota(jnp.int32, (OWNERS, OWNERS), 1)
    owner_row = owners[...]
    owner_column = jnp.sum(jnp.where(sub == lane, owner_row, 0), axis=1, keepdims=True)
    holder = jnp.sum(jnp.where(owner_column == lane, sub, 0), axis=0, keepdims=True)
    tile[2:3, :OWNERS] = jnp.minimum(holder, OWNERS - 1)
    load_masks.wait()
    tile[0:1, :OWNERS] = places_of(masks[block_a])
    tile[1:2, :OWNERS] = places_of(masks[block_b])
    to_table = pltpu.make_async_copy(tile, table, small_sems.at[3])
    to_table.start()

    def regroup(first, count, matrix, at):
        for h in range(2):
            for c in range(COL_BLOCKS // 2):
                cols = pl.ds(2 * BLOCK * c, 2 * BLOCK)
                part = [
                    raw[pl.ds(pl.multiple_of((first + r) * OWNERS + h * HALF, HALF), HALF), cols]
                    for r in range(count)
                ]
                found = jnp.dot(
                    matrix[...], jnp.concatenate(part, axis=0), preferred_element_type=jnp.float32
                )
                for u in range(2):
                    by_expert[2 * c + u, HALF * h : HALF * (h + 1), at : at + 8, :] = found[
                        :, BLOCK * u : BLOCK * (u + 1)
                    ].reshape(HALF, 8, BLOCK)

    for i in range(3):
        load(phase + 2 * i).wait()
        load(phase + 2 * i + 1).wait()
        regroup(4 * phase + 8 * i, 8, turn, 8 * i)
    load(6 - 6 * phase).wait()
    regroup(24 - 24 * phase, 4, turn_rest, MAIN)
    to_table.wait()

    row = lax.broadcasted_iota(jnp.int32, (MAIN + 8, BLOCK), 0)
    row = row + jnp.where(row < MAIN, 4 * phase, -28 * phase)
    in_a = row < split
    straight = (lax.broadcasted_iota(jnp.int32, (8, BLOCK), 0) // 4) == phase

    def pack(t):
        e = table[2, owner_at(me, t)]
        code_a, code_b = table[0, e], table[1, e]
        mains, rests = [], []
        for k in range(CARRIED):
            rows = jnp.where(in_a, by_expert[column_of(code_a, k), e], by_expert[column_of(code_b, k), e])
            mains.append(rows[:MAIN])
            rests.append(rows[MAIN:])
        left_a = jnp.where(straight, rests[0], pltpu.roll(rests[1], 4, 0))
        left_b = jnp.where(straight, rests[2], pltpu.roll(rests[3], 4, 0))
        send[t] = jnp.concatenate(mains + [left_a, left_b], axis=0).astype(jnp.bfloat16)

    def to(t, gt):
        return pltpu.make_async_remote_copy(
            src_ref=send.at[t],
            dst_ref=recv.at[my_id],
            send_sem=send_sem,
            recv_sem=recv_sem,
            device_id=(gt, owner_at(me, t)),
            device_id_type=MESH,
        )

    pack(0)
    keep = pltpu.make_async_copy(send.at[0], recv.at[my_id], keep_sem)
    keep.start()
    pl.semaphore_wait(barrier, PEERS)
    to(0, 1 - g).start()

    def step(t, carry):
        pack(t)
        to(t, g).start()
        to(t, 1 - g).start()
        return carry

    lax.fori_loop(1, OWNERS, step, 0)

    mine = jnp.sum(jnp.where(owner_row[None] == me, masks[...], 0), axis=2, keepdims=True)
    mine = places_of(jnp.broadcast_to(mine, (ROW_BLOCKS, COL_BLOCKS, BLOCK)))
    lane = lax.broadcasted_iota(jnp.int32, mine.shape, 2)
    block = lax.broadcasted_iota(jnp.int32, mine.shape, 0)
    own[...] = jnp.sum(jnp.where(lane == block, mine, 0), axis=0)

    load_scales.wait()
    load_codes.wait()
    keep.wait()
    sent = recv.at[pl.ds(0, PEERS)]
    pltpu.make_async_copy(sent, sent, send_sem).wait()
    pltpu.make_async_copy(sent, sent, recv_sem).wait()


def decode(own, scales, held, base, out, out_scales, change, peaks, made, out_sem):
    low = lax.broadcasted_iota(jnp.int32, (8, BLOCK), 0) < 4
    lane = lax.broadcasted_iota(jnp.int32, (COL_BLOCKS, BLOCK), 1)
    column = lax.broadcasted_iota(jnp.int32, (COL_BLOCKS, BLOCK), 0)
    per_set = GROUPS * OWNERS // SETS
    pairs = per_set // 2

    def one_set(s, found):
        rows_of = [[[] for k in range(CARRIED)] for r in range(PER_SET)]
        for r in range(PER_SET):
            a = s * PER_SET + r
            here = pl.ds(pl.multiple_of(a * BLOCK, BLOCK), BLOCK)
            made[here, :] = jnp.zeros((BLOCK, COL_BLOCKS * BLOCK), jnp.bfloat16)
        for r in range(PER_SET):
            a = s * PER_SET + r
            here = pl.ds(pl.multiple_of(a * BLOCK, BLOCK), BLOCK)
            code = own[0, a]
            first, last = BLOCK * r, BLOCK * (r + 1)
            parts = [[] for k in range(CARRIED)]
            for m in range(first // PAIR, (last + PAIR - 1) // PAIR):
                even = held[s * per_set + 2 * m].astype(jnp.float32)
                odd = held[s * per_set + 2 * m + 1].astype(jnp.float32)
                for k in range(CARRIED):
                    at = CARRIED * MAIN + 8 * (k // 2)
                    rest_even, rest_odd = even[at : at + 8], odd[at : at + 8]
                    if k % 2 == 0:
                        middle = jnp.where(low, rest_even, rest_odd)
                    else:
                        middle = pltpu.roll(jnp.where(low, rest_odd, rest_even), 4, 0)
                    whole = jnp.concatenate(
                        [even[MAIN * k : MAIN * (k + 1)], middle, odd[MAIN * k : MAIN * (k + 1)]], axis=0
                    )
                    parts[k].append(whole[max(first - PAIR * m, 0) : min(last - PAIR * m, PAIR)])
            for k in range(CARRIED):
                col = column_of(code, k)
                at = pl.ds(pl.multiple_of(col * BLOCK, BLOCK), BLOCK)
                diff = jnp.concatenate(parts[k], axis=0) - base[here, at].astype(jnp.float32) * scales[col, a]
                change[r * CARRIED + k] = diff
                peaks[r * CARRIED + k] = jnp.max(jnp.abs(diff).reshape(16, 8, BLOCK), axis=0)
        peak = jnp.max(jnp.max(peaks[...], axis=1, keepdims=True), axis=2, keepdims=True) + 1e-06
        inverse = 1.0 / peak
        for r in range(PER_SET):
            a = s * PER_SET + r
            here = pl.ds(pl.multiple_of(a * BLOCK, BLOCK), BLOCK)
            code = own[0, a]
            for k in range(CARRIED):
                i = r * CARRIED + k
                col = column_of(code, k)
                at = pl.ds(pl.multiple_of(col * BLOCK, BLOCK), BLOCK)
                made[here, at] = (change[i] * inverse[i]).astype(jnp.bfloat16)
                found = jnp.where((lane == a) & (column == col), peak[i], found)
            pltpu.make_async_copy(made.at[here], out.at[here], out_sem).start()
        return found

    found = lax.fori_loop(0, SETS, one_set, jnp.zeros((COL_BLOCKS, BLOCK), jnp.float32))
    out_scales[...] = found[:, :ROW_BLOCKS].astype(jnp.bfloat16)
    pltpu.make_async_copy(made, out, out_sem).wait()


def body(new_weights, owner_map, block_mask, base_codes, base_scale):
    weights = new_weights.transpose(1, 0, 2).reshape(SHARD * OWNERS, COL_BLOCKS * BLOCK)
    mask = block_mask.transpose(1, 2, 0)
    smem = pl.BlockSpec(memory_space=pltpu.SMEM)
    vmem = pl.BlockSpec(memory_space=pltpu.VMEM)
    inputs = [
        pltpu.with_memory_space_constraint(x, pltpu.HBM)
        for x in (owner_map.reshape(1, OWNERS), mask, base_scale[0].T, base_codes[0], weights)
    ]
    anywhere = pl.BlockSpec(memory_space=pl.ANY)

    recv, own, scales, codes = pl.pallas_call(
        exchange,
        out_shape=(
            jax.ShapeDtypeStruct((GROUPS * OWNERS, PIECE, BLOCK), jnp.bfloat16),
            jax.ShapeDtypeStruct((1, BLOCK), jnp.int32),
            jax.ShapeDtypeStruct((COL_BLOCKS, ROW_BLOCKS), jnp.float32),
            jax.ShapeDtypeStruct(base_codes.shape[1:], jnp.bfloat16),
        ),
        in_specs=[anywhere] * 5,
        out_specs=(anywhere, vmem, anywhere, anywhere),
        scratch_shapes=[
            pltpu.VMEM((1, OWNERS), jnp.int32),
            pltpu.VMEM(mask.shape, jnp.int32),
            pltpu.VMEM((8, BLOCK), jnp.int32),
            pltpu.SMEM((8, BLOCK), jnp.int32),
            pltpu.VMEM(weights.shape, jnp.bfloat16),
            pltpu.VMEM((COL_BLOCKS, OWNERS, MAIN + 8, BLOCK), jnp.float32),
            pltpu.VMEM((256, 256), jnp.bfloat16),
            pltpu.VMEM((256, BLOCK), jnp.bfloat16),
            pltpu.VMEM((OWNERS, PIECE, BLOCK), jnp.bfloat16),
            pltpu.SemaphoreType.DMA((5,)),
            pltpu.SemaphoreType.DMA((CHUNKS,)),
            pltpu.SemaphoreType.DMA,
            pltpu.SemaphoreType.DMA,
            pltpu.SemaphoreType.DMA,
        ],
        compiler_params=pltpu.CompilerParams(
            collective_id=0, has_side_effects=True, vmem_limit_bytes=32 * 2**20
        ),
        name="exchange",
    )(*inputs)

    deltas, delta_scales = pl.pallas_call(
        decode,
        out_shape=(
            jax.ShapeDtypeStruct(base_codes.shape[1:], jnp.bfloat16),
            jax.ShapeDtypeStruct((COL_BLOCKS, ROW_BLOCKS), jnp.bfloat16),
        ),
        in_specs=[smem, smem, vmem, vmem],
        out_specs=(anywhere, vmem),
        scratch_shapes=[
            pltpu.VMEM((PER_SET * CARRIED, BLOCK, BLOCK), jnp.float32),
            pltpu.VMEM((PER_SET * CARRIED, 8, BLOCK), jnp.float32),
            pltpu.VMEM(base_codes.shape[1:], jnp.bfloat16),
            pltpu.SemaphoreType.DMA,
        ],
        compiler_params=pltpu.CompilerParams(vmem_limit_bytes=24 * 2**20),
        name="decode",
    )(own, scales, recv, codes)
    return deltas[None, None], delta_scales.T[None, None]


def solution(mesh):
    return jax.shard_map(
        body,
        mesh=mesh,
        in_specs=(
            P(None, ("group", "dev"), None),
            P(),
            P(),
            P("dev", None, None),
            P("dev", None, None),
        ),
        out_specs=(P("group", "dev", None, None), P("group", "dev", None, None)),
        check_vma=False,
    )
```

```python
import jax
import jax.numpy as jnp
from jax import lax
from jax.experimental import pallas as pl
from jax.experimental.pallas import tpu as pltpu
from jax.sharding import PartitionSpec as P

BLOCK = 128
MESH = pl.DeviceIdType.MESH
OWNERS = 64
GROUPS = 2
PEERS = GROUPS * OWNERS - 1
SHARD = 28
ROW_BLOCKS = 28
COL_BLOCKS = 8
CARRIED = 4
MAIN = 24
PIECE = SHARD * CARRIED
PAIR = 2 * SHARD
SETS = 4
PER_SET = ROW_BLOCKS // SETS
CHUNKS = 7
CHUNK = 4 * OWNERS
HALF = OWNERS // 2


def owner_at(me, t):
    core, y, zl, x = me % 2, (me // 2) % 4, (me // 8) % 2, me // 16
    a, b, e = t % 4, (t // 4) % 4, t // 16
    v = (a + e) % 4
    x = (x + a) % 4
    y = (y + b + 4 - a) % 4
    zl = (zl + v % 2) % 2
    core = (core + v // 2) % 2
    return ((x * 2 + zl) * 4 + y) * 2 + core


def places_of(mask):
    axis = mask.ndim - 2
    column = lax.broadcasted_iota(jnp.int32, mask.shape, axis)
    upto = mask
    for step in (1, 2, 4):
        upto = upto + jnp.where(column >= step, pltpu.roll(upto, step, axis), 0)
    value = jnp.zeros_like(mask)
    for k in range(CARRIED):
        value = value + jnp.where(upto == k + 1, column << (3 * k), 0)
    return jnp.sum(jnp.where(mask > 0, value, 0), axis=axis, keepdims=True)


def column_of(code, k):
    return (code >> (3 * k)) & 7


def exchange(
    owner_map, mask, scales, codes, weights, recv, own, scales_out, codes_out,
    owners, masks, tile, table, raw, by_expert, turn, turn_rest, send,
    small_sems, load_sems, keep_sem, send_sem, recv_sem,
):
    g = lax.axis_index("group")
    me = lax.axis_index("dev")
    my_id = g * OWNERS + me
    first_row = my_id * SHARD
    block_a = first_row // BLOCK
    block_b = jnp.minimum(block_a + 1, ROW_BLOCKS - 1)
    split = (block_a + 1) * BLOCK - first_row
    phase = me % 2

    barrier = pltpu.get_barrier_semaphore()

    def load(i):
        rows = pl.ds(pl.multiple_of(i * CHUNK, CHUNK), CHUNK)
        return pltpu.make_async_copy(weights.at[rows], raw.at[rows], load_sems.at[i])

    load_owners = pltpu.make_async_copy(owner_map, owners, small_sems.at[0])
    load_masks = pltpu.make_async_copy(mask, masks, small_sems.at[1])
    load_scales = pltpu.make_async_copy(scales, scales_out, small_sems.at[2])
    load_codes = pltpu.make_async_copy(codes, codes_out, small_sems.at[4])
    load_owners.start()
    load_masks.start()
    for i in range(CHUNKS):
        load(i).start()
    for other in range(GROUPS * OWNERS):

        @pl.when(other != my_id)
        def _():
            pl.semaphore_signal(
                barrier, inc=1, device_id=(other // OWNERS, other % OWNERS), device_id_type=MESH
            )

    load_scales.start()
    load_codes.start()

    to_row = lax.broadcasted_iota(jnp.int32, (256, 256), 0)
    from_row = lax.broadcasted_iota(jnp.int32, (256, 256), 1)
    same = (to_row // 8 == from_row % HALF) & (to_row % 8 == from_row // HALF)
    turn[...] = jnp.where(same, 1.0, 0.0).astype(jnp.bfloat16)
    same = (to_row // 8 == from_row % HALF) & (to_row % 8 == from_row // HALF + 4 * phase)
    turn_rest[...] = jnp.where(same, 1.0, 0.0).astype(jnp.bfloat16)[:, :BLOCK]

    load_owners.wait()
    sub = lax.broadcasted_iota(jnp.int32, (OWNERS, OWNERS), 0)
    lane = lax.broadcasted_iota(jnp.int32, (OWNERS, OWNERS), 1)
    owner_row = owners[...]
    owner_column = jnp.sum(jnp.where(sub == lane, owner_row, 0), axis=1, keepdims=True)
    holder = jnp.sum(jnp.where(owner_column == lane, sub, 0), axis=0, keepdims=True)
    tile[2:3, :OWNERS] = jnp.minimum(holder, OWNERS - 1)
    load_masks.wait()
    tile[0:1, :OWNERS] = places_of(masks[block_a])
    tile[1:2, :OWNERS] = places_of(masks[block_b])
    to_table = pltpu.make_async_copy(tile, table, small_sems.at[3])
    to_table.start()

    def regroup(first, count, matrix, at):
        for h in range(2):
            for c in range(COL_BLOCKS // 2):
                cols = pl.ds(2 * BLOCK * c, 2 * BLOCK)
                part = [
                    raw[pl.ds(pl.multiple_of((first + r) * OWNERS + h * HALF, HALF), HALF), cols]
                    for r in range(count)
                ]
                found = jnp.dot(
                    matrix[...], jnp.concatenate(part, axis=0), preferred_element_type=jnp.float32
                )
                for u in range(2):
                    by_expert[2 * c + u, HALF * h : HALF * (h + 1), at : at + 8, :] = found[
                        :, BLOCK * u : BLOCK * (u + 1)
                    ].reshape(HALF, 8, BLOCK)

    for i in range(3):
        load(phase + 2 * i).wait()
        load(phase + 2 * i + 1).wait()
        regroup(4 * phase + 8 * i, 8, turn, 8 * i)
    load(6 - 6 * phase).wait()
    regroup(24 - 24 * phase, 4, turn_rest, MAIN)
    to_table.wait()

    row = lax.broadcasted_iota(jnp.int32, (MAIN + 8, BLOCK), 0)
    row = row + jnp.where(row < MAIN, 4 * phase, -28 * phase)
    in_a = row < split
    straight = (lax.broadcasted_iota(jnp.int32, (8, BLOCK), 0) // 4) == phase

    def pack(t):
        e = table[2, owner_at(me, t)]
        code_a, code_b = table[0, e], table[1, e]
        mains, rests = [], []
        for k in range(CARRIED):
            rows = jnp.where(in_a, by_expert[column_of(code_a, k), e], by_expert[column_of(code_b, k), e])
            mains.append(rows[:MAIN])
            rests.append(rows[MAIN:])
        left_a = jnp.where(straight, rests[0], pltpu.roll(rests[1], 4, 0))
        left_b = jnp.where(straight, rests[2], pltpu.roll(rests[3], 4, 0))
        send[t] = jnp.concatenate(mains + [left_a, left_b], axis=0).astype(jnp.bfloat16)

    def to(t, gt):
        return pltpu.make_async_remote_copy(
            src_ref=send.at[t],
            dst_ref=recv.at[my_id],
            send_sem=send_sem,
            recv_sem=recv_sem,
            device_id=(gt, owner_at(me, t)),
            device_id_type=MESH,
        )

    pack(0)
    keep = pltpu.make_async_copy(send.at[0], recv.at[my_id], keep_sem)
    keep.start()
    pl.semaphore_wait(barrier, PEERS)
    to(0, 1 - g).start()

    def step(t, carry):
        pack(t)
        to(t, 1 - g).start()
        to(t, g).start()
        return carry

    lax.fori_loop(1, OWNERS, step, 0)

    mine = jnp.sum(jnp.where(owner_row[None] == me, masks[...], 0), axis=2, keepdims=True)
    mine = places_of(jnp.broadcast_to(mine, (ROW_BLOCKS, COL_BLOCKS, BLOCK)))
    lane = lax.broadcasted_iota(jnp.int32, mine.shape, 2)
    block = lax.broadcasted_iota(jnp.int32, mine.shape, 0)
    own[...] = jnp.sum(jnp.where(lane == block, mine, 0), axis=0)

    load_scales.wait()
    load_codes.wait()
    keep.wait()
    sent = recv.at[pl.ds(0, PEERS)]
    pltpu.make_async_copy(sent, sent, send_sem).wait()
    pltpu.make_async_copy(sent, sent, recv_sem).wait()


def decode(own, scales, held, base, out, out_scales, change, peaks, made, out_sem):
    low = lax.broadcasted_iota(jnp.int32, (8, BLOCK), 0) < 4
    lane = lax.broadcasted_iota(jnp.int32, (COL_BLOCKS, BLOCK), 1)
    column = lax.broadcasted_iota(jnp.int32, (COL_BLOCKS, BLOCK), 0)
    per_set = GROUPS * OWNERS // SETS
    pairs = per_set // 2

    def one_set(s, found):
        rows_of = [[[] for k in range(CARRIED)] for r in range(PER_SET)]
        for r in range(PER_SET):
            a = s * PER_SET + r
            here = pl.ds(pl.multiple_of(a * BLOCK, BLOCK), BLOCK)
            made[here, :] = jnp.zeros((BLOCK, COL_BLOCKS * BLOCK), jnp.bfloat16)
        for r in range(PER_SET):
            a = s * PER_SET + r
            here = pl.ds(pl.multiple_of(a * BLOCK, BLOCK), BLOCK)
            code = own[0, a]
            first, last = BLOCK * r, BLOCK * (r + 1)
            parts = [[] for k in range(CARRIED)]
            for m in range(first // PAIR, (last + PAIR - 1) // PAIR):
                even = held[s * per_set + 2 * m].astype(jnp.float32)
                odd = held[s * per_set + 2 * m + 1].astype(jnp.float32)
                for k in range(CARRIED):
                    at = CARRIED * MAIN + 8 * (k // 2)
                    rest_even, rest_odd = even[at : at + 8], odd[at : at + 8]
                    if k % 2 == 0:
                        middle = jnp.where(low, rest_even, rest_odd)
                    else:
                        middle = pltpu.roll(jnp.where(low, rest_odd, rest_even), 4, 0)
                    whole = jnp.concatenate(
                        [even[MAIN * k : MAIN * (k + 1)], middle, odd[MAIN * k : MAIN * (k + 1)]], axis=0
                    )
                    parts[k].append(whole[max(first - PAIR * m, 0) : min(last - PAIR * m, PAIR)])
            for k in range(CARRIED):
                col = column_of(code, k)
                at = pl.ds(pl.multiple_of(col * BLOCK, BLOCK), BLOCK)
                diff = jnp.concatenate(parts[k], axis=0) - base[here, at].astype(jnp.float32) * scales[col, a]
                change[r * CARRIED + k] = diff
                peaks[r * CARRIED + k] = jnp.max(jnp.abs(diff).reshape(16, 8, BLOCK), axis=0)
        peak = jnp.max(jnp.max(peaks[...], axis=1, keepdims=True), axis=2, keepdims=True) + 1e-06
        inverse = 1.0 / peak
        for r in range(PER_SET):
            a = s * PER_SET + r
            here = pl.ds(pl.multiple_of(a * BLOCK, BLOCK), BLOCK)
            code = own[0, a]
            for k in range(CARRIED):
                i = r * CARRIED + k
                col = column_of(code, k)
                at = pl.ds(pl.multiple_of(col * BLOCK, BLOCK), BLOCK)
                made[here, at] = (change[i] * inverse[i]).astype(jnp.bfloat16)
                found = jnp.where((lane == a) & (column == col), peak[i], found)
            pltpu.make_async_copy(made.at[here], out.at[here], out_sem).start()
        return found

    found = lax.fori_loop(0, SETS, one_set, jnp.zeros((COL_BLOCKS, BLOCK), jnp.float32))
    out_scales[...] = found[:, :ROW_BLOCKS].astype(jnp.bfloat16)
    pltpu.make_async_copy(made, out, out_sem).wait()


def body(new_weights, owner_map, block_mask, base_codes, base_scale):
    weights = new_weights.transpose(1, 0, 2).reshape(SHARD * OWNERS, COL_BLOCKS * BLOCK)
    mask = block_mask.transpose(1, 2, 0)
    smem = pl.BlockSpec(memory_space=pltpu.SMEM)
    vmem = pl.BlockSpec(memory_space=pltpu.VMEM)
    inputs = [
        pltpu.with_memory_space_constraint(x, pltpu.HBM)
        for x in (owner_map.reshape(1, OWNERS), mask, base_scale[0].T, base_codes[0], weights)
    ]
    anywhere = pl.BlockSpec(memory_space=pl.ANY)

    recv, own, scales, codes = pl.pallas_call(
        exchange,
        out_shape=(
            jax.ShapeDtypeStruct((GROUPS * OWNERS, PIECE, BLOCK), jnp.bfloat16),
            jax.ShapeDtypeStruct((1, BLOCK), jnp.int32),
            jax.ShapeDtypeStruct((COL_BLOCKS, ROW_BLOCKS), jnp.float32),
            jax.ShapeDtypeStruct(base_codes.shape[1:], jnp.bfloat16),
        ),
        in_specs=[anywhere] * 5,
        out_specs=(anywhere, vmem, anywhere, anywhere),
        scratch_shapes=[
            pltpu.VMEM((1, OWNERS), jnp.int32),
            pltpu.VMEM(mask.shape, jnp.int32),
            pltpu.VMEM((8, BLOCK), jnp.int32),
            pltpu.SMEM((8, BLOCK), jnp.int32),
            pltpu.VMEM(weights.shape, jnp.bfloat16),
            pltpu.VMEM((COL_BLOCKS, OWNERS, MAIN + 8, BLOCK), jnp.float32),
            pltpu.VMEM((256, 256), jnp.bfloat16),
            pltpu.VMEM((256, BLOCK), jnp.bfloat16),
            pltpu.VMEM((OWNERS, PIECE, BLOCK), jnp.bfloat16),
            pltpu.SemaphoreType.DMA((5,)),
            pltpu.SemaphoreType.DMA((CHUNKS,)),
            pltpu.SemaphoreType.DMA,
            pltpu.SemaphoreType.DMA,
            pltpu.SemaphoreType.DMA,
        ],
        compiler_params=pltpu.CompilerParams(
            collective_id=0, has_side_effects=True, vmem_limit_bytes=32 * 2**20
        ),
        name="exchange",
    )(*inputs)

    deltas, delta_scales = pl.pallas_call(
        decode,
        out_shape=(
            jax.ShapeDtypeStruct(base_codes.shape[1:], jnp.bfloat16),
            jax.ShapeDtypeStruct((COL_BLOCKS, ROW_BLOCKS), jnp.bfloat16),
        ),
        in_specs=[smem, smem, vmem, vmem],
        out_specs=(anywhere, vmem),
        scratch_shapes=[
            pltpu.VMEM((PER_SET * CARRIED, BLOCK, BLOCK), jnp.float32),
            pltpu.VMEM((PER_SET * CARRIED, 8, BLOCK), jnp.float32),
            pltpu.VMEM(base_codes.shape[1:], jnp.bfloat16),
            pltpu.SemaphoreType.DMA,
        ],
        compiler_params=pltpu.CompilerParams(vmem_limit_bytes=24 * 2**20),
        name="decode",
    )(own, scales, recv, codes)
    return deltas[None, None], delta_scales.T[None, None]


def solution(mesh):
    return jax.shard_map(
        body,
        mesh=mesh,
        in_specs=(
            P(None, ("group", "dev"), None),
            P(),
            P(),
            P("dev", None, None),
            P("dev", None, None),
        ),
        out_specs=(P("group", "dev", None, None), P("group", "dev", None, None)),
        check_vma=False,
    )
```

```python
import jax
import jax.numpy as jnp
from jax import lax
from jax.experimental import pallas as pl
from jax.experimental.pallas import tpu as pltpu
from jax.sharding import PartitionSpec as P

BLOCK = 128
MESH = pl.DeviceIdType.MESH
OWNERS = 64
GROUPS = 2
PEERS = GROUPS * OWNERS - 1
SHARD = 28
ROW_BLOCKS = 28
COL_BLOCKS = 8
CARRIED = 4
MAIN = 24
PIECE = SHARD * CARRIED
PAIR = 2 * SHARD
SETS = 4
PER_SET = ROW_BLOCKS // SETS
CHUNKS = 7
CHUNK = 4 * OWNERS
HALF = OWNERS // 2


def owner_at(me, t):
    core, y, zl, x = me % 2, (me // 2) % 4, (me // 8) % 2, me // 16
    a, b, e = t % 4, (t // 4) % 4, t // 16
    v = (a + e) % 4
    x = (x + a) % 4
    y = (y + b + 4 - a) % 4
    zl = (zl + v % 2) % 2
    core = (core + v // 2) % 2
    return ((x * 2 + zl) * 4 + y) * 2 + core


def places_of(mask):
    axis = mask.ndim - 2
    column = lax.broadcasted_iota(jnp.int32, mask.shape, axis)
    upto = mask
    for step in (1, 2, 4):
        upto = upto + jnp.where(column >= step, pltpu.roll(upto, step, axis), 0)
    value = jnp.zeros_like(mask)
    for k in range(CARRIED):
        value = value + jnp.where(upto == k + 1, column << (3 * k), 0)
    return jnp.sum(jnp.where(mask > 0, value, 0), axis=axis, keepdims=True)


def column_of(code, k):
    return (code >> (3 * k)) & 7


def exchange(
    owner_map, mask, scales, codes, weights, recv, own, base, blank,
    owners, masks, tile, table, own_table, scale_table, raw, by_expert, turn, turn_rest, send, by_column, made, zeros,
    small_sems, load_sems, code_sems, base_sem, blank_sem, keep_sem, send_sem, recv_sem,
):
    g = lax.axis_index("group")
    me = lax.axis_index("dev")
    my_id = g * OWNERS + me
    first_row = my_id * SHARD
    block_a = first_row // BLOCK
    block_b = jnp.minimum(block_a + 1, ROW_BLOCKS - 1)
    split = (block_a + 1) * BLOCK - first_row
    phase = me % 2

    barrier = pltpu.get_barrier_semaphore()

    def load(i):
        rows = pl.ds(pl.multiple_of(i * CHUNK, CHUNK), CHUNK)
        return pltpu.make_async_copy(weights.at[rows], raw.at[rows], load_sems.at[i])

    load_owners = pltpu.make_async_copy(owner_map, owners, small_sems.at[0])
    load_masks = pltpu.make_async_copy(mask, masks, small_sems.at[1])
    load_scales = pltpu.make_async_copy(scales, scale_table, small_sems.at[2])
    load_codes = [
        pltpu.make_async_copy(codes.at[:, :, pl.ds(BLOCK * c, BLOCK)], by_column.at[c], code_sems.at[c])
        for c in range(COL_BLOCKS)
    ]
    load_owners.start()
    load_masks.start()
    for i in range(CHUNKS):
        load(i).start()
    for other in range(GROUPS * OWNERS):

        @pl.when(other != my_id)
        def _():
            pl.semaphore_signal(
                barrier, inc=1, device_id=(other // OWNERS, other % OWNERS), device_id_type=MESH
            )

    load_scales.start()
    for copy in load_codes:
        copy.start()

    to_row = lax.broadcasted_iota(jnp.int32, (256, 256), 0)
    from_row = lax.broadcasted_iota(jnp.int32, (256, 256), 1)
    same = (to_row // 8 == from_row % HALF) & (to_row % 8 == from_row // HALF)
    turn[...] = jnp.where(same, 1.0, 0.0).astype(jnp.bfloat16)
    same = (to_row // 8 == from_row % HALF) & (to_row % 8 == from_row // HALF + 4 * phase)
    turn_rest[...] = jnp.where(same, 1.0, 0.0).astype(jnp.bfloat16)[:, :BLOCK]

    load_owners.wait()
    sub = lax.broadcasted_iota(jnp.int32, (OWNERS, OWNERS), 0)
    lane = lax.broadcasted_iota(jnp.int32, (OWNERS, OWNERS), 1)
    owner_row = owners[...]
    owner_column = jnp.sum(jnp.where(sub == lane, owner_row, 0), axis=1, keepdims=True)
    holder = jnp.sum(jnp.where(owner_column == lane, sub, 0), axis=0, keepdims=True)
    tile[2:3, :OWNERS] = jnp.minimum(holder, OWNERS - 1)
    load_masks.wait()
    tile[0:1, :OWNERS] = places_of(masks[block_a])
    tile[1:2, :OWNERS] = places_of(masks[block_b])
    to_table = pltpu.make_async_copy(tile, table, small_sems.at[3])
    to_table.start()

    def regroup(first, count, matrix, at):
        for h in range(2):
            for c in range(COL_BLOCKS // 2):
                cols = pl.ds(2 * BLOCK * c, 2 * BLOCK)
                part = [
                    raw[pl.ds(pl.multiple_of((first + r) * OWNERS + h * HALF, HALF), HALF), cols]
                    for r in range(count)
                ]
                found = jnp.dot(
                    matrix[...], jnp.concatenate(part, axis=0), preferred_element_type=jnp.float32
                )
                for u in range(2):
                    by_expert[2 * c + u, HALF * h : HALF * (h + 1), at : at + 8, :] = found[
                        :, BLOCK * u : BLOCK * (u + 1)
                    ].reshape(HALF, 8, BLOCK)

    for i in range(3):
        load(phase + 2 * i).wait()
        load(phase + 2 * i + 1).wait()
        regroup(4 * phase + 8 * i, 8, turn, 8 * i)
    load(6 - 6 * phase).wait()
    regroup(24 - 24 * phase, 4, turn_rest, MAIN)
    to_table.wait()

    row = lax.broadcasted_iota(jnp.int32, (MAIN + 8, BLOCK), 0)
    row = row + jnp.where(row < MAIN, 4 * phase, -28 * phase)
    in_a = row < split
    straight = (lax.broadcasted_iota(jnp.int32, (8, BLOCK), 0) // 4) == phase

    def pack(t):
        e = table[2, owner_at(me, t)]
        code_a, code_b = table[0, e], table[1, e]
        mains, rests = [], []
        for k in range(CARRIED):
            rows = jnp.where(in_a, by_expert[column_of(code_a, k), e], by_expert[column_of(code_b, k), e])
            mains.append(rows[:MAIN])
            rests.append(rows[MAIN:])
        left_a = jnp.where(straight, rests[0], pltpu.roll(rests[1], 4, 0))
        left_b = jnp.where(straight, rests[2], pltpu.roll(rests[3], 4, 0))
        send[t] = jnp.concatenate(mains + [left_a, left_b], axis=0).astype(jnp.bfloat16)

    def to(t, gt):
        return pltpu.make_async_remote_copy(
            src_ref=send.at[t],
            dst_ref=recv.at[my_id],
            send_sem=send_sem,
            recv_sem=recv_sem,
            device_id=(gt, owner_at(me, t)),
            device_id_type=MESH,
        )

    pack(0)
    keep = pltpu.make_async_copy(send.at[0], recv.at[my_id], keep_sem)
    keep.start()
    pl.semaphore_wait(barrier, PEERS)
    to(0, 1 - g).start()

    def step(t, carry):
        pack(t)
        to(t, 1 - g).start()
        to(t, g).start()
        return carry

    lax.fori_loop(1, OWNERS, step, 0)

    mine = jnp.sum(jnp.where(owner_row[None] == me, masks[...], 0), axis=2, keepdims=True)
    mine = places_of(jnp.broadcast_to(mine, (ROW_BLOCKS, COL_BLOCKS, BLOCK)))
    lane = lax.broadcasted_iota(jnp.int32, mine.shape, 2)
    block = lax.broadcasted_iota(jnp.int32, mine.shape, 0)
    own[...] = jnp.sum(jnp.where(lane == block, mine, 0), axis=0)

    to_own = pltpu.make_async_copy(own, own_table, small_sems.at[4])
    to_own.start()
    zeros[...] = jnp.zeros_like(zeros)

    def clear(a):
        rows = pl.ds(pl.multiple_of(a * BLOCK, BLOCK), BLOCK)
        return pltpu.make_async_copy(zeros, blank.at[rows], blank_sem)

    def clear_one(a, carry):
        clear(a).start()
        return carry

    lax.fori_loop(0, ROW_BLOCKS, clear_one, 0)
    load_scales.wait()
    for copy in load_codes:
        copy.wait()
    to_own.wait()

    def base_rows(a, carry):
        for k in range(CARRIED):
            col = column_of(own_table[0, a], k)
            made[a * CARRIED + k] = by_column[col, a].astype(jnp.float32) * scale_table[col, a]
        return carry

    lax.fori_loop(0, ROW_BLOCKS, base_rows, 0)
    to_base = pltpu.make_async_copy(made, base, base_sem)
    to_base.start()
    to_base.wait()
    pltpu.make_async_copy(blank, blank, blank_sem).wait()
    keep.wait()
    sent = recv.at[pl.ds(0, PEERS)]
    pltpu.make_async_copy(sent, sent, send_sem).wait()
    pltpu.make_async_copy(sent, sent, recv_sem).wait()


def decode(own, held, base, blank, out, out_scales, made, change, peaks, table, found_scales, own_sem, scale_sem, out_sem):
    to_table = pltpu.make_async_copy(own, table, own_sem)
    to_table.start()
    low = lax.broadcasted_iota(jnp.int32, (8, BLOCK), 0) < 4
    lane = lax.broadcasted_iota(jnp.int32, (COL_BLOCKS, BLOCK), 1)
    column = lax.broadcasted_iota(jnp.int32, (COL_BLOCKS, BLOCK), 0)
    per_set = GROUPS * OWNERS // SETS
    pairs = per_set // 2

    def one_set(s, found):
        for r in range(PER_SET):
            a = s * PER_SET + r
            first, last = BLOCK * r, BLOCK * (r + 1)
            parts = [[] for k in range(CARRIED)]
            for m in range(first // PAIR, (last + PAIR - 1) // PAIR):
                even = held[s * per_set + 2 * m].astype(jnp.float32)
                odd = held[s * per_set + 2 * m + 1].astype(jnp.float32)
                for k in range(CARRIED):
                    at = CARRIED * MAIN + 8 * (k // 2)
                    rest_even, rest_odd = even[at : at + 8], odd[at : at + 8]
                    if k % 2 == 0:
                        middle = jnp.where(low, rest_even, rest_odd)
                    else:
                        middle = pltpu.roll(jnp.where(low, rest_odd, rest_even), 4, 0)
                    whole = jnp.concatenate(
                        [even[MAIN * k : MAIN * (k + 1)], middle, odd[MAIN * k : MAIN * (k + 1)]], axis=0
                    )
                    parts[k].append(whole[max(first - PAIR * m, 0) : min(last - PAIR * m, PAIR)])
            for k in range(CARRIED):
                diff = jnp.concatenate(parts[k], axis=0) - base[a * CARRIED + k]
                change[r * CARRIED + k] = diff
                peaks[r * CARRIED + k] = jnp.max(jnp.abs(diff).reshape(16, 8, BLOCK), axis=0)
        if isinstance(s, int) and s == 0:
            to_table.wait()
        peak = jnp.max(jnp.max(peaks[...], axis=1, keepdims=True), axis=2, keepdims=True) + 1e-06
        inverse = 1.0 / peak
        for r in range(PER_SET):
            a = s * PER_SET + r
            here = pl.ds(pl.multiple_of(a * BLOCK, BLOCK), BLOCK)
            code = table[0, a]
            for k in range(CARRIED):
                i = r * CARRIED + k
                col = column_of(code, k)
                at = pl.ds(pl.multiple_of(col * BLOCK, BLOCK), BLOCK)
                made[here, at] = (change[i] * inverse[i]).astype(jnp.bfloat16)
                found = jnp.where((lane == a) & (column == col), peak[i], found)
            pltpu.make_async_copy(made.at[here], out.at[here], out_sem).start()
        return found

    found = one_set(0, jnp.zeros((COL_BLOCKS, BLOCK), jnp.float32))
    found = lax.fori_loop(1, SETS, one_set, found)
    found_scales[...] = found[:, :ROW_BLOCKS].astype(jnp.bfloat16)
    to_scales = pltpu.make_async_copy(found_scales, out_scales, scale_sem)
    to_scales.start()
    pltpu.make_async_copy(made, out, out_sem).wait()
    to_scales.wait()


def body(new_weights, owner_map, block_mask, base_codes, base_scale):
    weights = new_weights.transpose(1, 0, 2).reshape(SHARD * OWNERS, COL_BLOCKS * BLOCK)
    mask = block_mask.transpose(1, 2, 0)
    smem = pl.BlockSpec(memory_space=pltpu.SMEM)
    vmem = pl.BlockSpec(memory_space=pltpu.VMEM)
    codes = base_codes[0].reshape(ROW_BLOCKS, BLOCK, COL_BLOCKS * BLOCK)
    inputs = [
        pltpu.with_memory_space_constraint(x, pltpu.HBM)
        for x in (owner_map.reshape(1, OWNERS), mask, base_scale[0].T, codes, weights)
    ]
    anywhere = pl.BlockSpec(memory_space=pl.ANY)

    recv, own, base, blank = pl.pallas_call(
        exchange,
        out_shape=(
            pltpu.VMEM((GROUPS * OWNERS, PIECE, BLOCK), jnp.bfloat16),
            pltpu.VMEM((1, BLOCK), jnp.int32),
            pltpu.VMEM((ROW_BLOCKS * CARRIED, BLOCK, BLOCK), jnp.float32),
            pltpu.VMEM(base_codes.shape[1:], jnp.bfloat16),
        ),
        in_specs=[anywhere] * 5,
        out_specs=(anywhere, vmem, anywhere, anywhere),
        scratch_shapes=[
            pltpu.VMEM((1, OWNERS), jnp.int32),
            pltpu.VMEM(mask.shape, jnp.int32),
            pltpu.VMEM((8, BLOCK), jnp.int32),
            pltpu.SMEM((8, BLOCK), jnp.int32),
            pltpu.SMEM((1, BLOCK), jnp.int32),
            pltpu.SMEM((COL_BLOCKS, ROW_BLOCKS), jnp.float32),
            pltpu.VMEM(weights.shape, jnp.bfloat16),
            pltpu.VMEM((COL_BLOCKS, OWNERS, MAIN + 8, BLOCK), jnp.float32),
            pltpu.VMEM((256, 256), jnp.bfloat16),
            pltpu.VMEM((256, BLOCK), jnp.bfloat16),
            pltpu.VMEM((OWNERS, PIECE, BLOCK), jnp.bfloat16),
            pltpu.VMEM((COL_BLOCKS, ROW_BLOCKS, BLOCK, BLOCK), jnp.bfloat16),
            pltpu.VMEM((ROW_BLOCKS * CARRIED, BLOCK, BLOCK), jnp.float32),
            pltpu.VMEM((BLOCK, COL_BLOCKS * BLOCK), jnp.bfloat16),
            pltpu.SemaphoreType.DMA((5,)),
            pltpu.SemaphoreType.DMA((CHUNKS,)),
            pltpu.SemaphoreType.DMA((COL_BLOCKS,)),
            pltpu.SemaphoreType.DMA,
            pltpu.SemaphoreType.DMA,
            pltpu.SemaphoreType.DMA,
            pltpu.SemaphoreType.DMA,
            pltpu.SemaphoreType.DMA,
        ],
        compiler_params=pltpu.CompilerParams(
            collective_id=0, has_side_effects=True, vmem_limit_bytes=40 * 2**20
        ),
        name="exchange",
    )(*inputs)

    deltas, delta_scales, _ = pl.pallas_call(
        decode,
        out_shape=(
            jax.ShapeDtypeStruct(base_codes.shape[1:], jnp.bfloat16),
            jax.ShapeDtypeStruct((COL_BLOCKS, ROW_BLOCKS), jnp.bfloat16),
            pltpu.VMEM(base_codes.shape[1:], jnp.bfloat16),
        ),
        in_specs=[anywhere, vmem, vmem, vmem],
        out_specs=(anywhere, anywhere, vmem),
        input_output_aliases={3: 2},
        scratch_shapes=[
            pltpu.VMEM((PER_SET * CARRIED, BLOCK, BLOCK), jnp.float32),
            pltpu.VMEM((PER_SET * CARRIED, 8, BLOCK), jnp.float32),
            pltpu.SMEM((1, BLOCK), jnp.int32),
            pltpu.VMEM((COL_BLOCKS, ROW_BLOCKS), jnp.bfloat16),
            pltpu.SemaphoreType.DMA,
            pltpu.SemaphoreType.DMA,
            pltpu.SemaphoreType.DMA,
        ],
        compiler_params=pltpu.CompilerParams(vmem_limit_bytes=24 * 2**20),
        name="decode",
    )(*(pltpu.with_memory_space_constraint(x, pltpu.VMEM) for x in (own, recv, base, blank)))
    return deltas[None, None], delta_scales.T[None, None]


def solution(mesh):
    return jax.shard_map(
        body,
        mesh=mesh,
        in_specs=(
            P(None, ("group", "dev"), None),
            P(),
            P(),
            P("dev", None, None),
            P("dev", None, None),
        ),
        out_specs=(P("group", "dev", None, None), P("group", "dev", None, None)),
        check_vma=False,
    )
```

```python
import jax
import jax.numpy as jnp
from jax import lax
from jax.experimental import pallas as pl
from jax.experimental.pallas import tpu as pltpu
from jax.sharding import PartitionSpec as P

BLOCK = 128
MESH = pl.DeviceIdType.MESH
OWNERS = 64
GROUPS = 2
PEERS = GROUPS * OWNERS - 1
SHARD = 28
ROW_BLOCKS = 28
COL_BLOCKS = 8
CARRIED = 4
MAIN = 24
PIECE = SHARD * CARRIED
PAIR = 2 * SHARD
SETS = 4
PER_SET = ROW_BLOCKS // SETS
CHUNKS = 7
CHUNK = 4 * OWNERS
HALF = OWNERS // 2


def owner_at(me, t):
    core, y, zl, x = me % 2, (me // 2) % 4, (me // 8) % 2, me // 16
    a, b, e = t % 4, (t // 4) % 4, t // 16
    v = (a + e) % 4
    x = (x + a) % 4
    y = (y + b + 4 - a) % 4
    zl = (zl + v % 2) % 2
    core = (core + v // 2) % 2
    return ((x * 2 + zl) * 4 + y) * 2 + core


def places_of(mask):
    axis = mask.ndim - 2
    column = lax.broadcasted_iota(jnp.int32, mask.shape, axis)
    upto = mask
    for step in (1, 2, 4):
        upto = upto + jnp.where(column >= step, pltpu.roll(upto, step, axis), 0)
    value = jnp.zeros_like(mask)
    for k in range(CARRIED):
        value = value + jnp.where(upto == k + 1, column << (3 * k), 0)
    return jnp.sum(jnp.where(mask > 0, value, 0), axis=axis, keepdims=True)


def column_of(code, k):
    return (code >> (3 * k)) & 7


def exchange(
    owner_map, mask, scales, codes, weights, recv, own, base, blank,
    owners, masks, tile, table, own_table, scale_table, raw, by_expert, turn, turn_rest, send, by_column, made, zeros,
    small_sems, load_sems, code_sems, base_sem, blank_sem, keep_sem, send_sem, recv_sem,
):
    g = lax.axis_index("group")
    me = lax.axis_index("dev")
    my_id = g * OWNERS + me
    first_row = my_id * SHARD
    block_a = first_row // BLOCK
    block_b = jnp.minimum(block_a + 1, ROW_BLOCKS - 1)
    split = (block_a + 1) * BLOCK - first_row
    phase = me % 2

    barrier = pltpu.get_barrier_semaphore()

    def load(i):
        rows = pl.ds(pl.multiple_of(i * CHUNK, CHUNK), CHUNK)
        return pltpu.make_async_copy(weights.at[rows], raw.at[rows], load_sems.at[i])

    load_owners = pltpu.make_async_copy(owner_map, owners, small_sems.at[0])
    load_masks = pltpu.make_async_copy(mask, masks, small_sems.at[1])
    load_scales = pltpu.make_async_copy(scales, scale_table, small_sems.at[2])
    load_codes = [
        pltpu.make_async_copy(codes.at[:, :, pl.ds(BLOCK * c, BLOCK)], by_column.at[c], code_sems.at[c])
        for c in range(COL_BLOCKS)
    ]
    load_owners.start()
    load_masks.start()
    for i in range(CHUNKS):
        load(i).start()
    for other in range(GROUPS * OWNERS):

        @pl.when(other != my_id)
        def _():
            pl.semaphore_signal(
                barrier, inc=1, device_id=(other // OWNERS, other % OWNERS), device_id_type=MESH
            )

    load_scales.start()
    for copy in load_codes:
        copy.start()

    to_row = lax.broadcasted_iota(jnp.int32, (256, 256), 0)
    from_row = lax.broadcasted_iota(jnp.int32, (256, 256), 1)
    same = (to_row // 8 == from_row % HALF) & (to_row % 8 == from_row // HALF)
    turn[...] = jnp.where(same, 1.0, 0.0).astype(jnp.bfloat16)
    same = (to_row // 8 == from_row % HALF) & (to_row % 8 == from_row // HALF + 4 * phase)
    turn_rest[...] = jnp.where(same, 1.0, 0.0).astype(jnp.bfloat16)[:, :BLOCK]

    load_owners.wait()
    sub = lax.broadcasted_iota(jnp.int32, (OWNERS, OWNERS), 0)
    lane = lax.broadcasted_iota(jnp.int32, (OWNERS, OWNERS), 1)
    owner_row = owners[...]
    owner_column = jnp.sum(jnp.where(sub == lane, owner_row, 0), axis=1, keepdims=True)
    holder = jnp.sum(jnp.where(owner_column == lane, sub, 0), axis=0, keepdims=True)
    tile[2:3, :OWNERS] = jnp.minimum(holder, OWNERS - 1)
    load_masks.wait()
    tile[0:1, :OWNERS] = places_of(masks[block_a])
    tile[1:2, :OWNERS] = places_of(masks[block_b])
    to_table = pltpu.make_async_copy(tile, table, small_sems.at[3])
    to_table.start()

    def regroup(first, count, matrix, at):
        for h in range(2):
            for c in range(COL_BLOCKS // 2):
                cols = pl.ds(2 * BLOCK * c, 2 * BLOCK)
                part = [
                    raw[pl.ds(pl.multiple_of((first + r) * OWNERS + h * HALF, HALF), HALF), cols]
                    for r in range(count)
                ]
                found = jnp.dot(
                    matrix[...], jnp.concatenate(part, axis=0), preferred_element_type=jnp.float32
                )
                for u in range(2):
                    by_expert[2 * c + u, HALF * h : HALF * (h + 1), at : at + 8, :] = found[
                        :, BLOCK * u : BLOCK * (u + 1)
                    ].reshape(HALF, 8, BLOCK)

    for i in range(3):
        load(phase + 2 * i).wait()
        load(phase + 2 * i + 1).wait()
        regroup(4 * phase + 8 * i, 8, turn, 8 * i)
    load(6 - 6 * phase).wait()
    regroup(24 - 24 * phase, 4, turn_rest, MAIN)
    to_table.wait()

    row = lax.broadcasted_iota(jnp.int32, (MAIN + 8, BLOCK), 0)
    row = row + jnp.where(row < MAIN, 4 * phase, -28 * phase)
    in_a = row < split
    straight = (lax.broadcasted_iota(jnp.int32, (8, BLOCK), 0) // 4) == phase

    def pack(t):
        e = table[2, owner_at(me, t)]
        code_a, code_b = table[0, e], table[1, e]
        mains, rests = [], []
        for k in range(CARRIED):
            rows = jnp.where(in_a, by_expert[column_of(code_a, k), e], by_expert[column_of(code_b, k), e])
            mains.append(rows[:MAIN])
            rests.append(rows[MAIN:])
        left_a = jnp.where(straight, rests[0], pltpu.roll(rests[1], 4, 0))
        left_b = jnp.where(straight, rests[2], pltpu.roll(rests[3], 4, 0))
        send[t] = jnp.concatenate(mains + [left_a, left_b], axis=0).astype(jnp.bfloat16)

    def to(t, gt):
        return pltpu.make_async_remote_copy(
            src_ref=send.at[t],
            dst_ref=recv.at[my_id],
            send_sem=send_sem,
            recv_sem=recv_sem,
            device_id=(gt, owner_at(me, t)),
            device_id_type=MESH,
        )

    pack(0)
    keep = pltpu.make_async_copy(send.at[0], recv.at[my_id], keep_sem)
    keep.start()
    pl.semaphore_wait(barrier, PEERS)
    to(0, 1 - g).start()

    def step(t, carry):
        pack(t)
        to(t, 1 - g).start()
        to(t, g).start()
        return carry

    lax.fori_loop(1, OWNERS, step, 0)

    mine = jnp.sum(jnp.where(owner_row[None] == me, masks[...], 0), axis=2, keepdims=True)
    mine = places_of(jnp.broadcast_to(mine, (ROW_BLOCKS, COL_BLOCKS, BLOCK)))
    lane = lax.broadcasted_iota(jnp.int32, mine.shape, 2)
    block = lax.broadcasted_iota(jnp.int32, mine.shape, 0)
    own[...] = jnp.sum(jnp.where(lane == block, mine, 0), axis=0)

    to_own = pltpu.make_async_copy(own, own_table, small_sems.at[4])
    to_own.start()
    zeros[...] = jnp.zeros_like(zeros)

    def clear(a):
        rows = pl.ds(pl.multiple_of(a * BLOCK, BLOCK), BLOCK)
        return pltpu.make_async_copy(zeros, blank.at[rows], blank_sem)

    def clear_one(a, carry):
        clear(a).start()
        return carry

    lax.fori_loop(0, ROW_BLOCKS, clear_one, 0)
    load_scales.wait()
    for copy in load_codes:
        copy.wait()
    to_own.wait()

    def base_rows(a, carry):
        for k in range(CARRIED):
            col = column_of(own_table[0, a], k)
            made[a * CARRIED + k] = by_column[col, a].astype(jnp.float32) * scale_table[col, a]
        return carry

    lax.fori_loop(0, ROW_BLOCKS, base_rows, 0)
    to_base = pltpu.make_async_copy(made, base, base_sem)
    to_base.start()
    to_base.wait()
    pltpu.make_async_copy(blank, blank, blank_sem).wait()
    keep.wait()
    sent = recv.at[pl.ds(0, PEERS)]
    pltpu.make_async_copy(sent, sent, send_sem).wait()
    pltpu.make_async_copy(sent, sent, recv_sem).wait()


def decode(own, held, base, blank, out, out_scales, made, change, peaks, table, own_sem, out_sem):
    to_table = pltpu.make_async_copy(own, table, own_sem)
    to_table.start()
    low = lax.broadcasted_iota(jnp.int32, (8, BLOCK), 0) < 4
    lane = lax.broadcasted_iota(jnp.int32, (COL_BLOCKS, BLOCK), 1)
    column = lax.broadcasted_iota(jnp.int32, (COL_BLOCKS, BLOCK), 0)
    per_set = GROUPS * OWNERS // SETS
    pairs = per_set // 2

    def one_set(s, found):
        for r in range(PER_SET):
            a = s * PER_SET + r
            first, last = BLOCK * r, BLOCK * (r + 1)
            parts = [[] for k in range(CARRIED)]
            for m in range(first // PAIR, (last + PAIR - 1) // PAIR):
                even = held[s * per_set + 2 * m].astype(jnp.float32)
                odd = held[s * per_set + 2 * m + 1].astype(jnp.float32)
                for k in range(CARRIED):
                    at = CARRIED * MAIN + 8 * (k // 2)
                    rest_even, rest_odd = even[at : at + 8], odd[at : at + 8]
                    if k % 2 == 0:
                        middle = jnp.where(low, rest_even, rest_odd)
                    else:
                        middle = pltpu.roll(jnp.where(low, rest_odd, rest_even), 4, 0)
                    whole = jnp.concatenate(
                        [even[MAIN * k : MAIN * (k + 1)], middle, odd[MAIN * k : MAIN * (k + 1)]], axis=0
                    )
                    parts[k].append(whole[max(first - PAIR * m, 0) : min(last - PAIR * m, PAIR)])
            for k in range(CARRIED):
                diff = jnp.concatenate(parts[k], axis=0) - base[a * CARRIED + k]
                change[r * CARRIED + k] = diff
                peaks[r * CARRIED + k] = jnp.max(jnp.abs(diff).reshape(16, 8, BLOCK), axis=0)
        if isinstance(s, int) and s == 0:
            to_table.wait()
        peak = jnp.max(jnp.max(peaks[...], axis=1, keepdims=True), axis=2, keepdims=True) + 1e-06
        inverse = 1.0 / peak
        for r in range(PER_SET):
            a = s * PER_SET + r
            here = pl.ds(pl.multiple_of(a * BLOCK, BLOCK), BLOCK)
            code = table[0, a]
            for k in range(CARRIED):
                i = r * CARRIED + k
                col = column_of(code, k)
                at = pl.ds(pl.multiple_of(col * BLOCK, BLOCK), BLOCK)
                made[here, at] = (change[i] * inverse[i]).astype(jnp.bfloat16)
                found = jnp.where((lane == a) & (column == col), peak[i], found)
            pltpu.make_async_copy(made.at[here], out.at[here], out_sem).start()
        return found

    found = one_set(0, jnp.zeros((COL_BLOCKS, BLOCK), jnp.float32))
    found = lax.fori_loop(1, SETS, one_set, found)
    out_scales[...] = found[:, :ROW_BLOCKS].astype(jnp.bfloat16)
    pltpu.make_async_copy(made, out, out_sem).wait()


def body(new_weights, owner_map, block_mask, base_codes, base_scale):
    weights = new_weights.transpose(1, 0, 2).reshape(SHARD * OWNERS, COL_BLOCKS * BLOCK)
    mask = block_mask.transpose(1, 2, 0)
    smem = pl.BlockSpec(memory_space=pltpu.SMEM)
    vmem = pl.BlockSpec(memory_space=pltpu.VMEM)
    codes = base_codes[0].reshape(ROW_BLOCKS, BLOCK, COL_BLOCKS * BLOCK)
    inputs = [
        pltpu.with_memory_space_constraint(x, pltpu.HBM)
        for x in (owner_map.reshape(1, OWNERS), mask, base_scale[0].T, codes, weights)
    ]
    anywhere = pl.BlockSpec(memory_space=pl.ANY)

    recv, own, base, blank = pl.pallas_call(
        exchange,
        out_shape=(
            pltpu.VMEM((GROUPS * OWNERS, PIECE, BLOCK), jnp.bfloat16),
            pltpu.VMEM((1, BLOCK), jnp.int32),
            pltpu.VMEM((ROW_BLOCKS * CARRIED, BLOCK, BLOCK), jnp.float32),
            pltpu.VMEM(base_codes.shape[1:], jnp.bfloat16),
        ),
        in_specs=[anywhere] * 5,
        out_specs=(anywhere, vmem, anywhere, anywhere),
        scratch_shapes=[
            pltpu.VMEM((1, OWNERS), jnp.int32),
            pltpu.VMEM(mask.shape, jnp.int32),
            pltpu.VMEM((8, BLOCK), jnp.int32),
            pltpu.SMEM((8, BLOCK), jnp.int32),
            pltpu.SMEM((1, BLOCK), jnp.int32),
            pltpu.SMEM((COL_BLOCKS, ROW_BLOCKS), jnp.float32),
            pltpu.VMEM(weights.shape, jnp.bfloat16),
            pltpu.VMEM((COL_BLOCKS, OWNERS, MAIN + 8, BLOCK), jnp.float32),
            pltpu.VMEM((256, 256), jnp.bfloat16),
            pltpu.VMEM((256, BLOCK), jnp.bfloat16),
            pltpu.VMEM((OWNERS, PIECE, BLOCK), jnp.bfloat16),
            pltpu.VMEM((COL_BLOCKS, ROW_BLOCKS, BLOCK, BLOCK), jnp.bfloat16),
            pltpu.VMEM((ROW_BLOCKS * CARRIED, BLOCK, BLOCK), jnp.float32),
            pltpu.VMEM((BLOCK, COL_BLOCKS * BLOCK), jnp.bfloat16),
            pltpu.SemaphoreType.DMA((5,)),
            pltpu.SemaphoreType.DMA((CHUNKS,)),
            pltpu.SemaphoreType.DMA((COL_BLOCKS,)),
            pltpu.SemaphoreType.DMA,
            pltpu.SemaphoreType.DMA,
            pltpu.SemaphoreType.DMA,
            pltpu.SemaphoreType.DMA,
            pltpu.SemaphoreType.DMA,
        ],
        compiler_params=pltpu.CompilerParams(
            collective_id=0, has_side_effects=True, vmem_limit_bytes=40 * 2**20
        ),
        name="exchange",
    )(*inputs)

    deltas, delta_scales, _ = pl.pallas_call(
        decode,
        out_shape=(
            jax.ShapeDtypeStruct(base_codes.shape[1:], jnp.bfloat16),
            jax.ShapeDtypeStruct((COL_BLOCKS, ROW_BLOCKS), jnp.bfloat16),
            pltpu.VMEM(base_codes.shape[1:], jnp.bfloat16),
        ),
        in_specs=[anywhere, vmem, vmem, vmem],
        out_specs=(anywhere, vmem, vmem),
        input_output_aliases={3: 2},
        scratch_shapes=[
            pltpu.VMEM((PER_SET * CARRIED, BLOCK, BLOCK), jnp.float32),
            pltpu.VMEM((PER_SET * CARRIED, 8, BLOCK), jnp.float32),
            pltpu.SMEM((1, BLOCK), jnp.int32),
            pltpu.SemaphoreType.DMA,
            pltpu.SemaphoreType.DMA,
        ],
        compiler_params=pltpu.CompilerParams(vmem_limit_bytes=24 * 2**20),
        name="decode",
    )(*(pltpu.with_memory_space_constraint(x, pltpu.VMEM) for x in (own, recv, base, blank)))
    return deltas[None, None], delta_scales.T[None, None]


def solution(mesh):
    return jax.shard_map(
        body,
        mesh=mesh,
        in_specs=(
            P(None, ("group", "dev"), None),
            P(),
            P(),
            P("dev", None, None),
            P("dev", None, None),
        ),
        out_specs=(P("group", "dev", None, None), P("group", "dev", None, None)),
        check_vma=False,
    )
```
